32 devices in a mesh: rep: 4 (over y, x), table: 8 (over z, core).
Axes of the slice: x: 2, y: 2, z: 4, core: 2. Of those that a mesh axis runs over, the one named last changes fastest.
Arguments:
- cold_table: float32 [8192, 400], P('table'), may hold values from -3 to 3
- cold_state: float32 [8192], P('table'), may hold values from 0.05 to 1
- hot_table: float32 [1024, 400], P('table'), may hold values from -3 to 3
- hot_state: float32 [1024], P('table'), may hold values from 0.05 to 1
- relations: float32 [512, 400], replicated, may hold values from -2.5 to 2.5
- head_owner: int32 [16384, 1], P(('rep', 'table')), may hold values from 0 to 7; in each aligned block of 512 rows (0 to 511, 512 to 1023, ...) at most 128 rows name the same one
- head_row: int32 [16384], P(('rep', 'table')), may hold values from 0 to 1023
- edge_rel: int32 [16384], P(('rep', 'table')), may hold values from 0 to 511
- edge_tail: int32 [16384], P(('rep', 'table')), may hold values from 0 to 1023, as said below
- neg_ids: int32 [4, 64], P('rep', 'table'), may hold values from 0 to 1023
Outputs:
- new_cold_table: float32 [8192, 400], P('table')
- new_cold_state: float32 [8192], P('table')
- new_hot_table: float32 [1024, 400], P('table')
- new_hot_state: float32 [1024], P('table')
The draws below stay inside these ranges and needn't reach their ends.
Inputs may be any that keep to these rules, and one draw needn't show every extreme that they name: `head_owner`: among the edges of one device (aligned blocks of 512), no owner is named more than 128 times. `neg_ids`: column j names a row of the cold rows of table index j // 8. `edge_tail`: among the edges of one device (aligned blocks of 512), the tails that lie in one aligned block of 128 hot rows are at most 32 distinct rows, and in some such block exactly 32.
All inputs are finite; a program needn't handle non-finite values.
Results may differ from the reference program's by a relative error of at most 0.00045.
The reference program's roundings to bfloat16 on the way count: a program that leaves them out, or rounds other values in their place, can miss the bound.
Values may be sent and summed in bfloat16 or wider, within the bound.
A program may use at most 128 MiB of HBM per device.

```python
import math
import jax
import jax.numpy as jnp
import numpy as np
from jax import lax

D = 400
REL = 512
HOT_DEV = 128
TAIL_CAP = 32
COLD_DEV = 1024
EDGES_DEV = 512
NEG_DEV = 8
CAP = 128
HOT = 1024
COLD = 8192
NEG = 64
EDGES = 16384
N_REP = 4
N_TABLE = 8


def draw_edge_tail(key, part):
    blocks = EDGES // EDGES_DEV
    owner_count = HOT // HOT_DEV
    key_perm, key_owner, key_slot, key_full = jax.random.split(jax.random.fold_in(key, 7), 4)
    perm_keys = jax.random.split(key_perm, blocks * owner_count)
    chosen = jax.vmap(lambda single: jax.random.permutation(single, HOT_DEV)[:TAIL_CAP])(perm_keys)
    chosen = chosen.reshape(blocks, owner_count, TAIL_CAP).astype(jnp.int32)
    owner_ids = jax.random.randint(key_owner, (blocks, EDGES_DEV), 0, owner_count, dtype=jnp.int32)
    slot_ids = jax.random.randint(key_slot, (blocks, EDGES_DEV), 0, TAIL_CAP, dtype=jnp.int32)
    full_owner = jax.random.randint(key_full, (blocks, 1), 0, owner_count, dtype=jnp.int32)
    position = jnp.arange(EDGES_DEV, dtype=jnp.int32)[None, :]
    leading = position < TAIL_CAP
    owner_ids = jnp.where(leading, full_owner, owner_ids)
    slot_ids = jnp.where(leading, jnp.minimum(position, TAIL_CAP - 1), slot_ids)
    block_ids = jnp.arange(blocks, dtype=jnp.int32)[:, None]
    picked = chosen[block_ids, owner_ids, slot_ids]
    return (owner_ids * HOT_DEV + picked).reshape(EDGES).astype(jnp.int32)


def place_ends(entries, rng, smallest, largest):
    dims = entries.shape
    place = [jax.random.randint(jax.random.fold_in(rng, axis), (), 0, dims[axis]) for axis in range(len(dims))]
    entries = entries.at[tuple(place)].set(smallest)
    longest = dims.index(max(dims))
    place[longest] = (place[longest] + 1) % dims[longest]
    return entries.at[tuple(place)].set(largest)


def block_levels(stream_key, dims, shards, least, high):
    loudness = 1.0
    for dim, parts in shards:
        heights = jax.random.uniform(jax.random.fold_in(jax.random.fold_in(stream_key, 6), dim), (parts,), jnp.float32, least / len(shards), high / len(shards))
        loudness = loudness * jnp.repeat(jnp.exp(heights), dims[dim] // parts).reshape((-1,) + (1,) * (len(dims) - 1 - dim))
    return loudness


def shared_out(stream_key, own, number, rows, count, top, most, skew):
    ranking = jax.random.permutation(stream_key, count)
    heavy_load, ordinary = portions_of(count, rows * top, most, skew, True), portions_of(count, rows * top, most, skew, False)
    places = jnp.arange(count)

    def named(lengths, offset_by):
        used = int((lengths > 0).sum())
        fixed = max(1, used // 4)
        moved = fixed + (places - fixed + offset_by * (used - fixed)) % max(1, count - fixed)
        return jnp.zeros((count,), jnp.int32).at[ranking[jnp.where(places < fixed, places, moved)]].set(jnp.asarray(lengths, jnp.int32))

    lengths = jnp.where(number % 4 == 0, named(heavy_load, number // 4), named(ordinary, number - number // 4 - 1))
    mixed = jax.random.permutation(jax.random.fold_in(own, 3), count)
    giver, receiver = mixed[0:count // 2 * 2:2], mixed[1:count // 2 * 2:2]
    room = jnp.minimum(lengths[giver] - 1, most - lengths[receiver]) // 2
    room = jnp.where((giver == ranking[0]) | (receiver == ranking[0]) | (lengths[receiver] == 0), 0, jnp.maximum(room, 0))
    moved = jax.random.randint(jax.random.fold_in(own, 4), (count // 2,), 0, 1 << 20) % (room + 1)
    lengths = lengths.at[giver].add(-moved).at[receiver].add(moved)
    items = jnp.searchsorted(jnp.cumsum(lengths), jnp.arange(rows * top), side="right").astype(jnp.int32)
    listing = items.reshape(top, rows).T
    listing = listing[jax.random.permutation(jax.random.fold_in(own, 1), rows)]
    offset_by = jax.random.randint(jax.random.fold_in(own, 2), (rows, 1), 0, top)
    return jnp.take_along_axis(listing, (jnp.arange(top)[None, :] + offset_by) % top, axis=1)


def portions_of(count, total, most, lean, full):
    portions = [(1 << 20) // math.isqrt(rank ** lean) + 1 for rank in range(1, count + 1)]
    largest = most if full else min(most, max(-(-total // count), total * portions[0] // sum(portions)))
    least = 1 if total - largest >= count - 1 else 0
    counts, spare = [largest] + [least] * (count - 1), total - largest - least * (count - 1)
    while spare > 0:
        free = [i for i in range(1, count) if counts[i] < largest] or [i for i in range(1, count) if counts[i] < most]
        pool, left = sum([portions[i] for i in free]), spare
        for i in free:
            more = min(most - counts[i], max(1, left * portions[i] // pool), spare)
            counts[i] = counts[i] + more
            spare = spare - more
    return np.array(counts)


def scatter_about(key, extent, scale, reach, pieces=(), kind=jnp.bfloat16):
    entries = scale * jax.random.normal(key, extent, jnp.float32)
    if pieces:
        entries = entries * block_levels(key, extent, pieces, -0.22, 0.18)
    return jnp.clip(entries, -reach, reach).astype(kind)


def setup_inputs(seed: int = 0) -> dict:
    arg_keys = jax.random.split(jax.random.key(seed), 11)
    cold_table = scatter_about(arg_keys[0], (COLD, D), 0.5, 3.0, ((0, 8),), jnp.float32)
    cold_state = jnp.clip(jnp.exp(math.log(1.0) - 2.9957323 * jax.random.uniform(arg_keys[1], (COLD,), jnp.float32) ** block_levels(arg_keys[1], (COLD,), ((0, 8),), -0.2, 0.2)), 0.05, 1.0)
    hot_table = scatter_about(arg_keys[2], (HOT, D), 0.5, 3.0, ((0, 8),), jnp.float32)
    hot_state = jnp.clip(jnp.exp(math.log(1.0) - 2.9957323 * jax.random.uniform(arg_keys[3], (HOT,), jnp.float32) ** block_levels(arg_keys[3], (HOT,), ((0, 8),), -0.2, 0.2)), 0.05, 1.0)
    relations = scatter_about(arg_keys[4], (REL, D), 0.2, 2.5, (), jnp.float32)
    head_owner_keys = jax.random.split(jax.random.fold_in(arg_keys[5], 1), EDGES // EDGES_DEV)
    head_owner_turns = jax.random.permutation(jax.random.fold_in(arg_keys[5], 3), EDGES // EDGES_DEV)
    head_owner = jax.vmap(lambda own, number: shared_out(jax.random.fold_in(arg_keys[5], 2), own, number, EDGES_DEV, N_TABLE, 1, CAP, 2))(head_owner_keys, head_owner_turns).reshape((EDGES, 1))
    head_row = place_ends(jax.random.randint(arg_keys[6], (EDGES,), 0, COLD_DEV), jax.random.fold_in(arg_keys[6], 1), 0, COLD_DEV - 1).astype(jnp.int32)
    edge_rel = place_ends(jax.random.randint(arg_keys[7], (EDGES,), 0, REL), jax.random.fold_in(arg_keys[7], 1), 0, REL - 1).astype(jnp.int32)
    edge_tail = draw_edge_tail(jax.random.fold_in(arg_keys[10], 71), 0)
    neg_ids = place_ends(jax.random.randint(arg_keys[9], (N_REP, NEG), 0, COLD_DEV), jax.random.fold_in(arg_keys[9], 1), 0, COLD_DEV - 1).astype(jnp.int32)
    return {"cold_table": cold_table, "cold_state": cold_state, "hot_table": hot_table, "hot_state": hot_state, "relations": relations, "head_owner": head_owner, "head_row": head_row, "edge_rel": edge_rel, "edge_tail": edge_tail, "neg_ids": neg_ids}


learn_rate = 0.5

def with_relation(relation, vector):
    half_width = vector.shape[1] // 2
    v_re, v_im = (vector[:, :half_width], vector[:, half_width:])
    r_re, r_im = (relation[:, :half_width], relation[:, half_width:])
    return jnp.concatenate([v_re * r_re - v_im * r_im, v_re * r_im + v_im * r_re], axis=1)

def against_relation(relation, vector):
    half_width = vector.shape[1] // 2
    v_re, v_im = (vector[:, :half_width], vector[:, half_width:])
    r_re, r_im = (relation[:, :half_width], relation[:, half_width:])
    return jnp.concatenate([r_re * v_re + r_im * v_im, r_re * v_im - r_im * v_re], axis=1)

def edge_terms(head_vec, relation, tail_vec, negatives, live_mask):
    head_f = head_vec.astype(jnp.float32)
    tail_f = tail_vec.astype(jnp.float32)
    queries = with_relation(relation, head_f)
    probes = against_relation(relation, tail_f)
    positive = lax.optimization_barrier(jnp.sum(queries * tail_f, axis=1))
    query_b = queries.astype(jnp.bfloat16)
    probe_b = probes.astype(jnp.bfloat16)
    tail_scores = jnp.dot(query_b, negatives.T, preferred_element_type=jnp.float32)
    head_scores = jnp.dot(probe_b, negatives.T, preferred_element_type=jnp.float32)
    pos_weight = -jax.nn.sigmoid(-positive) * live_mask
    tail_weight = (jax.nn.sigmoid(tail_scores) * live_mask[:, None]).astype(jnp.bfloat16)
    head_weight = (jax.nn.sigmoid(head_scores) * live_mask[:, None]).astype(jnp.bfloat16)
    tail_mix = jnp.dot(tail_weight, negatives, preferred_element_type=jnp.float32)
    head_mix = jnp.dot(head_weight, negatives, preferred_element_type=jnp.float32)
    head_grad = against_relation(relation, pos_weight[:, None] * tail_f + tail_mix).astype(jnp.bfloat16)
    tail_grad = with_relation(relation, pos_weight[:, None] * head_f + head_mix)
    neg_grad = jnp.dot(tail_weight.T, query_b, preferred_element_type=jnp.float32) + jnp.dot(head_weight.T, probe_b, preferred_element_type=jnp.float32)
    return (head_grad, tail_grad, neg_grad)

def adagrad(weights, state, grad):
    new_state = state + lax.optimization_barrier(jnp.mean(grad * grad, axis=1))
    return (weights - learn_rate * grad / jnp.sqrt(new_state)[:, None], new_state)

def reference(cold_table, cold_state, hot_table, hot_state, relations, head_owner, head_row, edge_rel, edge_tail, neg_ids):
    cold_bf = cold_table.astype(jnp.bfloat16)
    hot_bf = hot_table.astype(jnp.bfloat16)
    head_ids = (head_owner[:, 0] * COLD_DEV + head_row).astype(jnp.int32)
    shard_base = (jnp.arange(NEG, dtype=jnp.int32) // NEG_DEV * COLD_DEV).astype(jnp.int32)
    live_mask = jnp.ones((EDGES_DEV,), jnp.float32)

    def accumulate(totals, block_idx):
        cold_grad, hot_grad = totals
        replica = block_idx // N_TABLE
        start = (block_idx * EDGES_DEV).astype(jnp.int32)
        heads = lax.dynamic_slice_in_dim(head_ids, start, EDGES_DEV)
        rel_ids = lax.dynamic_slice_in_dim(edge_rel, start, EDGES_DEV)
        tails = lax.dynamic_slice_in_dim(edge_tail, start, EDGES_DEV)
        neg_rows = (lax.dynamic_index_in_dim(neg_ids, replica, 0, keepdims=False) + shard_base).astype(jnp.int32)
        negatives = cold_bf[neg_rows]
        head_grad, tail_grad, neg_grad = edge_terms(cold_bf[heads], relations[rel_ids], hot_bf[tails], negatives, live_mask)
        cold_grad = cold_grad.at[heads].add(head_grad.astype(jnp.float32))
        cold_grad = cold_grad.at[neg_rows].add(neg_grad)
        hot_grad = hot_grad.at[tails].add(tail_grad)
        return ((cold_grad, hot_grad), None)
    start_totals = (jnp.zeros(cold_table.shape, jnp.float32), jnp.zeros(hot_table.shape, jnp.float32))
    (cold_grad, hot_grad), unused = lax.scan(accumulate, start_totals, jnp.arange(N_REP * N_TABLE, dtype=jnp.int32))
    new_cold_table, new_cold_state = adagrad(cold_table, cold_state, cold_grad)
    new_hot_table, new_hot_state = adagrad(hot_table, hot_state, hot_grad)
    return (new_cold_table, new_cold_state, new_hot_table, new_hot_state)
```

```python
import functools

import jax
import jax.numpy as jnp
from jax import lax
from jax.experimental import pallas as pl
from jax.experimental.pallas import tpu as pltpu
from jax.sharding import PartitionSpec as P

learn_rate = 0.5


def with_relation(relation, vector):
    half_width = vector.shape[1] // 2
    v_re, v_im = (vector[:, :half_width], vector[:, half_width:])
    r_re, r_im = (relation[:, :half_width], relation[:, half_width:])
    return jnp.concatenate([v_re * r_re - v_im * r_im, v_re * r_im + v_im * r_re], axis=1)


def against_relation(relation, vector):
    half_width = vector.shape[1] // 2
    v_re, v_im = (vector[:, :half_width], vector[:, half_width:])
    r_re, r_im = (relation[:, :half_width], relation[:, half_width:])
    return jnp.concatenate([r_re * v_re + r_im * v_im, r_re * v_im - r_im * v_re], axis=1)


def edge_terms(head_vec, relation, tail_vec, negatives, live_mask):
    contract = (((1,), (1,)), ((), ()))
    across = (((0,), (0,)), ((), ()))
    head_f = head_vec.astype(jnp.float32)
    tail_f = tail_vec.astype(jnp.float32)
    queries = with_relation(relation, head_f)
    probes = against_relation(relation, tail_f)
    positive = jnp.sum(queries * tail_f, axis=1)
    query_b = queries.astype(jnp.bfloat16)
    probe_b = probes.astype(jnp.bfloat16)
    tail_scores = lax.dot_general(query_b, negatives, contract, preferred_element_type=jnp.float32)
    head_scores = lax.dot_general(probe_b, negatives, contract, preferred_element_type=jnp.float32)
    pos_weight = -jax.nn.sigmoid(-positive) * live_mask
    tail_weight = (jax.nn.sigmoid(tail_scores) * live_mask[:, None]).astype(jnp.bfloat16)
    head_weight = (jax.nn.sigmoid(head_scores) * live_mask[:, None]).astype(jnp.bfloat16)
    tail_mix = jnp.dot(tail_weight, negatives, preferred_element_type=jnp.float32)
    head_mix = jnp.dot(head_weight, negatives, preferred_element_type=jnp.float32)
    head_grad = against_relation(relation, pos_weight[:, None] * tail_f + tail_mix).astype(
        jnp.bfloat16
    )
    tail_grad = with_relation(relation, pos_weight[:, None] * head_f + head_mix)
    neg_grad = lax.dot_general(
        tail_weight, query_b, across, preferred_element_type=jnp.float32
    ) + lax.dot_general(head_weight, probe_b, across, preferred_element_type=jnp.float32)
    return (head_grad, tail_grad, neg_grad)


def adagrad(weights, state, grad):
    new_state = state + jnp.mean(grad * grad, axis=1)
    return (weights - learn_rate * grad / jnp.sqrt(new_state)[:, None], new_state)


def per_device(
    cold_table,
    cold_state,
    hot_table,
    hot_state,
    relations,
    head_owner,
    head_row,
    edge_rel,
    edge_tail,
    neg_ids,
):
    n_table = lax.axis_size("table")
    edge_count = head_row.shape[0]
    capacity = 2 * edge_count // n_table
    slot_total = n_table * capacity
    feature_width = cold_table.shape[1]
    cold_bf = cold_table.astype(jnp.bfloat16)
    hot_bf = hot_table.astype(jnp.bfloat16)
    local_negs = cold_bf[neg_ids[0]]
    hot_all, negatives = (
        lax.all_gather(hot_bf, "table", axis=0, tiled=True),
        lax.all_gather(local_negs, "table", axis=0, tiled=True),
    )
    owners = head_owner[:, 0]
    onehot = (owners[:, None] == jnp.arange(n_table, dtype=jnp.int32)[None, :]).astype(jnp.int32)
    position = jnp.arange(edge_count)
    before = (position[:, None] > position[None, :]).astype(jnp.bfloat16)
    counts = jnp.dot(before, onehot.astype(jnp.bfloat16), preferred_element_type=jnp.float32)
    slot_rank = jnp.sum(counts.astype(jnp.int32) * onehot, axis=1)
    slot_ids = owners * capacity + slot_rank
    cold_grad = jnp.zeros(cold_table.shape, jnp.float32)
    records = jnp.stack([head_row, edge_rel, edge_tail, jnp.ones_like(head_row)])
    packed = jnp.zeros((4, slot_total), jnp.int32).at[:, slot_ids].set(records)
    arrived = lax.all_to_all(
        packed.reshape(4, n_table, capacity), "table", split_axis=1, concat_axis=1, tiled=True
    )
    arrived = arrived.reshape(4, slot_total)
    row_ids, rel_ids, tail_ids, live_ids = (arrived[0], arrived[1], arrived[2], arrived[3])
    tail_live = live_ids.astype(jnp.float32)
    head_grad, tail_grad, neg_grad = edge_terms(
        cold_bf[row_ids], relations[rel_ids], hot_all[tail_ids], negatives, tail_live
    )
    cold_grad = cold_grad.at[row_ids].add(head_grad.astype(jnp.float32))
    hot_grad = jnp.zeros((hot_all.shape[0], feature_width), jnp.float32).at[tail_ids].add(tail_grad)
    hot_share, neg_share = (
        lax.psum_scatter(hot_grad, "table", scatter_dimension=0, tiled=True),
        lax.psum_scatter(neg_grad, "table", scatter_dimension=0, tiled=True),
    )
    cold_grad = cold_grad.at[neg_ids[0]].add(neg_share)
    cold_total, hot_total = lax.psum((cold_grad, hot_share), "rep")
    new_cold_table, new_cold_state = adagrad(cold_table, cold_state, cold_total)
    new_hot_table, new_hot_state = adagrad(hot_table, hot_state, hot_total)
    return (new_cold_table, new_cold_state, new_hot_table, new_hot_state)


def fits_kernel(n_rep, n_table, cold_rows, hot_rows, edges, neg_dev, width, rel_count):
    quarter = hot_rows // n_rep
    sizes = (n_rep, n_table, cold_rows, hot_rows, edges)
    return (
        all(s & (s - 1) == 0 for s in sizes)
        and 2 * edges // n_table == 128
        and n_table % 2 == 0
        and quarter % 16 == 0
        and quarter <= 256
        and neg_dev == 8
        and cold_rows % 128 == 0
        and cold_rows <= 4096
        and width % 2 == 0
        and width <= 512
        and n_table * hot_rows <= 4096
        and rel_count <= 1024
    )


def edge_kernel(
    dims,
    cold_ref,
    cstate_ref,
    hot_ref,
    hstate_ref,
    rel_ref,
    owner_ref,
    hrow_ref,
    erel_ref,
    etail_ref,
    nid_ref,
    cold_out,
    cstate_out,
    hot_out,
    hstate_out,
    coldbf,
    relparts,
    outbox,
    ids,
    hotall,
    negall,
    negbf,
    nidall,
    rowids,
    hgrad,
    hotgrad,
    hotrecv,
    hotsum,
    hotrecv2,
    hotfin,
    neggrad,
    negrecv,
    negfin,
    send1,
    recv1,
    send2,
    recv2,
    send3,
    recv3,
    send4,
    recv4,
    send5,
    recv5,
    send6,
    recv6,
    send7,
    recv7,
):
    n_rep, n_table = dims
    f32, bf16, i32 = jnp.float32, jnp.bfloat16, jnp.int32
    rep, tab = lax.axis_index("rep"), lax.axis_index("table")
    rows_c, width = cold_ref.shape
    half = width // 2
    edges = owner_ref.shape[0]
    rows_h = hot_ref.shape[0]
    quarter = rows_h // n_rep
    hot_total = n_table * rows_h
    rel_count = rel_ref.shape[0]
    padw = 256
    full = 2 * padw

    def spread(v):
        pad = jnp.zeros((v.shape[0], padw - half), v.dtype)
        return jnp.concatenate([v[:, :half], pad, v[:, half:], pad], axis=1)

    def close(v):
        return jnp.concatenate([v[:, :half], v[:, padw : padw + half]], axis=1)

    def dot(a, b, ca=1, cb=0):
        return lax.dot_general(a, b, (((ca,), (cb,)), ((), ())), preferred_element_type=f32)

    def hot_one(cond):
        return jnp.where(cond, 1.0, 0.0).astype(bf16)

    def to_table(step):
        return (rep, lax.rem(tab + step, n_table))

    def to_rep(step):
        return (lax.rem(rep + step, n_rep), tab)

    def remote(src, dst, ss, rs, dev):
        return pltpu.make_async_remote_copy(
            src_ref=src,
            dst_ref=dst,
            send_sem=ss,
            recv_sem=rs,
            device_id=dev,
            device_id_type=pl.DeviceIdType.MESH,
        )

    barrier = pltpu.get_barrier_semaphore()
    for s in range(1, n_table):
        pl.semaphore_signal(barrier, 1, device_id=to_table(s), device_id_type=pl.DeviceIdType.MESH)
    for s in range(1, n_rep):
        pl.semaphore_signal(barrier, 1, device_id=to_rep(s), device_id_type=pl.DeviceIdType.MESH)

    mine = hot_ref[pl.ds(pl.multiple_of(rep * quarter, quarter), quarter), :]
    hotall[rep, tab] = spread(mine).astype(bf16)

    owner = owner_ref[...]
    lane = lax.broadcasted_iota(i32, (edges, 128), 1)
    owned = lane == owner
    owned_b = hot_one(owned)
    before = hot_one(
        lax.broadcasted_iota(i32, (edges, edges), 0) > lax.broadcasted_iota(i32, (edges, edges), 1)
    )
    rank = jnp.sum(jnp.where(owned, dot(before, owned_b), 0.0), axis=1, keepdims=True)
    slot = owner * 128 + rank.astype(i32)
    hrow, erel, etail = hrow_ref[...], erel_ref[...], etail_ref[...]
    t_block = etail // rows_h
    t_in = etail % rows_h
    t_group = (t_in // quarter) * n_table + t_block
    fields = [
        hrow // 32,
        hrow % 32,
        erel // 32,
        erel % 32,
        t_group,
        t_in % quarter,
        jnp.ones_like(hrow),
        jnp.zeros_like(hrow),
    ]
    records = jnp.concatenate([f.astype(f32) for f in fields], axis=0).astype(bf16)
    for o in range(n_table):
        place = hot_one(lane + o * 128 == slot)
        outbox[o] = dot(records, place)
    pl.semaphore_wait(barrier, n_table + n_rep - 2)
    ids[rep, tab] = outbox[tab]

    first = []
    for s in range(1, n_table):
        dev = to_table(s)
        first.append(remote(outbox.at[dev[1]], ids.at[rep, tab], send1.at[0, s], recv1.at[0, s], dev))
        first.append(remote(hotall.at[rep, tab], hotall.at[rep, tab], send1.at[1, s], recv1.at[1, s], dev))
    for c in first:
        c.start()

    coldbf[...] = spread(cold_ref[...]).astype(bf16)
    nid = nid_ref[...]
    pick = hot_one(lax.broadcasted_iota(i32, (8, rows_c), 1) == nid)
    negall[rep, tab] = dot(pick, coldbf[...])
    nidall[rep] = jnp.broadcast_to(nid.astype(f32), (8, 128))
    more = []
    for s in range(1, n_table):
        more.append(
            remote(negall.at[rep, tab], negall.at[rep, tab], send1.at[2, s], recv1.at[2, s], to_table(s))
        )
    for c in more:
        c.start()

    rel = spread(rel_ref[...])
    rel_a = rel.astype(bf16)
    rest = rel - rel_a.astype(f32)
    rel_b = rest.astype(bf16)
    relparts[0] = rel_a
    relparts[1] = rel_b
    relparts[2] = (rest - rel_b.astype(f32)).astype(bf16)
    hotgrad[...] = jnp.zeros_like(hotgrad)
    neggrad[...] = jnp.zeros_like(neggrad)

    for c in first + more:
        c.wait()

    second = []
    for s in range(1, n_rep):
        dev = to_rep(s)
        second.append(remote(hotall.at[rep], hotall.at[rep], send2.at[0, s], recv2.at[0, s], dev))
        second.append(remote(ids.at[rep], ids.at[rep], send2.at[1, s], recv2.at[1, s], dev))
        second.append(remote(negall.at[rep], negall.at[rep], send2.at[2, s], recv2.at[2, s], dev))
        second.append(remote(nidall.at[rep], nidall.at[rep], send2.at[3, s], recv2.at[3, s], dev))
    for c in second:
        c.start()
    for c in second:
        c.wait()
    negbf[...] = negall[...].reshape(n_rep, n_table * 8, full).astype(bf16)

    def with_rel(r, v):
        r_re, r_im, v_re, v_im = r[:, :padw], r[:, padw:], v[:, :padw], v[:, padw:]
        return jnp.concatenate([v_re * r_re - v_im * r_im, v_re * r_im + v_im * r_re], axis=1)

    def against_rel(r, v):
        r_re, r_im, v_re, v_im = r[:, :padw], r[:, padw:], v[:, :padw], v[:, padw:]
        return jnp.concatenate([r_re * v_re + r_im * v_im, r_re * v_im - r_im * v_re], axis=1)

    chunk = 256
    per = n_table * 128 // chunk

    def edges_of(q, own):
        def body(c, carry):
            f = jnp.concatenate([ids[q, 2 * c], ids[q, 2 * c + 1]], axis=1)
            g = f.T.astype(i32)
            f = f.astype(i32)
            row_row = f[0:1] * 32 + f[1:2]
            rowids[q, c] = row_row
            row_col = g[:, 0:1] * 32 + g[:, 1:2]
            rel_col = g[:, 2:3] * 32 + g[:, 3:4]
            tail_col = g[:, 4:5] * quarter + g[:, 5:6]
            live = g[:, 6:7].astype(f32)
            wide = lambda n: lax.broadcasted_iota(i32, (chunk, n), 1)
            head_v = dot(hot_one(wide(rows_c) == row_col), coldbf[...])
            tail_v = dot(hot_one(wide(hot_total) == tail_col), hotall[...].reshape(hot_total, full))
            pick_r = hot_one(wide(rel_count) == rel_col)
            r = dot(pick_r, relparts[0]) + dot(pick_r, relparts[1]) + dot(pick_r, relparts[2])
            neg = negbf[q]
            queries = with_rel(r, head_v)
            positive = jnp.sum(queries * tail_v, axis=1, keepdims=True)
            query_b = queries.astype(bf16)
            tail_w = (jax.nn.sigmoid(dot(query_b, neg, 1, 1)) * live).astype(bf16)
            pos_w = -jax.nn.sigmoid(-positive) * live
            hgrad[q, c] = against_rel(r, pos_w * tail_v + dot(tail_w, neg)).astype(bf16)
            if own:
                probe_b = against_rel(r, tail_v).astype(bf16)
                head_w = (jax.nn.sigmoid(dot(probe_b, neg, 1, 1)) * live).astype(bf16)
                tail_g = with_rel(r, pos_w * head_v + dot(head_w, neg))
                neg_g = dot(tail_w, query_b, 0, 0) + dot(head_w, probe_b, 0, 0)
                neggrad[...] += neg_g.reshape(n_table, 8, full)
                hi = tail_g.astype(bf16)
                lo = (tail_g - hi.astype(f32)).astype(bf16)
                tail_row = f[4:5] * quarter + f[5:6]
                put = hot_one(lax.broadcasted_iota(i32, (hot_total, chunk), 0) == tail_row)
                hotgrad[...] += (dot(put, hi) + dot(put, lo)).reshape(hotgrad.shape)
            return carry

        lax.fori_loop(0, per, body, 0)

    edges_of(rep, True)

    third = []
    for s in range(1, n_rep):
        dev = to_rep(s)
        third.append(remote(hotgrad.at[dev[0]], hotrecv.at[rep], send3.at[s], recv3.at[s], dev))
    for s in range(1, n_table):
        dev = to_table(s)
        third.append(remote(neggrad.at[dev[1]], negrecv.at[tab], send6.at[s], recv6.at[s], dev))
    for c in third:
        c.start()
    hotrecv[rep] = hotgrad[rep]
    negrecv[tab] = neggrad[tab]

    others = [lax.rem(rep + s, n_rep) for s in range(1, n_rep)]
    split = max(1, len(others) // 3)
    for q in others[:split]:
        edges_of(q, False)

    for c in third:
        c.wait()
    acc = hotrecv[0]
    for k in range(1, n_rep):
        acc = acc + hotrecv[k]
    hotsum[...] = acc
    nacc = negrecv[0]
    for k in range(1, n_table):
        nacc = nacc + negrecv[k]
    negfin[rep] = nacc
    fourth = []
    for s in range(1, n_table):
        dev = to_table(s)
        fourth.append(remote(hotsum.at[dev[1]], hotrecv2.at[tab], send4.at[s], recv4.at[s], dev))
    for s in range(1, n_rep):
        fourth.append(remote(negfin.at[rep], negfin.at[rep], send7.at[s], recv7.at[s], to_rep(s)))
    for c in fourth:
        c.start()
    hotrecv2[tab] = hotsum[tab]

    for q in others[split : 2 * split]:
        edges_of(q, False)

    for c in fourth:
        c.wait()
    acc = hotrecv2[0]
    for k in range(1, n_table):
        acc = acc + hotrecv2[k]
    hotfin[rep] = acc
    fifth = [remote(hotfin.at[rep], hotfin.at[rep], send5.at[s], recv5.at[s], to_rep(s)) for s in range(1, n_rep)]
    for c in fifth:
        c.start()

    for q in others[2 * split :]:
        edges_of(q, False)

    def step(weights, state, grad):
        new_state = state + jnp.sum(grad * grad, axis=1, keepdims=True) / width
        return weights - learn_rate * close(grad) / jnp.sqrt(new_state), new_state

    neg_total = negfin[...].reshape(n_rep * 8, full)
    neg_hi = neg_total.astype(bf16)
    neg_rest = neg_total - neg_hi.astype(f32)
    neg_mid = neg_rest.astype(bf16)
    neg_lo = (neg_rest - neg_mid.astype(f32)).astype(bf16)
    neg_col = nidall[...].reshape(n_rep * 8, 128).astype(i32)
    block = 128

    def finish(b, carry):
        start = pl.multiple_of(b * block, block)
        base = lax.broadcasted_iota(i32, (block, chunk), 0) + start
        grad = jnp.zeros((block, full), f32)
        for q in range(n_rep):
            for c in range(per):
                grad = grad + dot(hot_one(base == rowids[q, c]), hgrad[q, c])
        put = hot_one(lax.broadcasted_iota(i32, (n_rep * 8, block), 1) + start == neg_col)
        grad = grad + (dot(put, neg_hi, 0, 0) + dot(put, neg_mid, 0, 0) + dot(put, neg_lo, 0, 0))
        at = pl.ds(start, block)
        table, state = step(cold_ref[at, :], cstate_ref[at, :], grad)
        cold_out[at, :] = table
        cstate_out[at, :] = state
        return carry

    lax.fori_loop(0, rows_c // block, finish, 0)

    for c in fifth:
        c.wait()
    table, state = step(hot_ref[...], hstate_ref[...], hotfin[...].reshape(rows_h, full))
    hot_out[...] = table
    hstate_out[...] = state


def per_device_kernel(
    cold_table,
    cold_state,
    hot_table,
    hot_state,
    relations,
    head_owner,
    head_row,
    edge_rel,
    edge_tail,
    neg_ids,
):
    n_rep, n_table = lax.axis_size("rep"), lax.axis_size("table")
    rows_c, width = cold_table.shape
    rows_h = hot_table.shape[0]
    edges = head_row.shape[0]
    rel_count = relations.shape[0]
    quarter = rows_h // n_rep
    full, chunk = 512, 256
    per = n_table * 128 // chunk
    f32, bf16 = jnp.float32, jnp.bfloat16
    dma = pltpu.SemaphoreType.DMA
    vmem = pl.BlockSpec(memory_space=pltpu.VMEM)
    outs = pl.pallas_call(
        functools.partial(edge_kernel, (n_rep, n_table)),
        out_shape=[
            jax.ShapeDtypeStruct((rows_c, width), f32),
            jax.ShapeDtypeStruct((rows_c, 1), f32),
            jax.ShapeDtypeStruct((rows_h, width), f32),
            jax.ShapeDtypeStruct((rows_h, 1), f32),
        ],
        in_specs=[vmem] * 10,
        out_specs=[vmem] * 4,
        scratch_shapes=[
            pltpu.VMEM((rows_c, full), bf16),
            pltpu.VMEM((3, rel_count, full), bf16),
            pltpu.VMEM((n_table, 8, 128), f32),
            pltpu.VMEM((n_rep, n_table, 8, 128), f32),
            pltpu.VMEM((n_rep, n_table, quarter, full), bf16),
            pltpu.VMEM((n_rep, n_table, 8, full), f32),
            pltpu.VMEM((n_rep, n_table * 8, full), bf16),
            pltpu.VMEM((n_rep, 8, 128), f32),
            pltpu.VMEM((n_rep, per, 1, chunk), jnp.int32),
            pltpu.VMEM((n_rep, per, chunk, full), bf16),
            pltpu.VMEM((n_rep, n_table, quarter, full), f32),
            pltpu.VMEM((n_rep, n_table, quarter, full), f32),
            pltpu.VMEM((n_table, quarter, full), f32),
            pltpu.VMEM((n_table, quarter, full), f32),
            pltpu.VMEM((n_rep, quarter, full), f32),
            pltpu.VMEM((n_table, 8, full), f32),
            pltpu.VMEM((n_table, 8, full), f32),
            pltpu.VMEM((n_rep, 8, full), f32),
            dma((3, n_table)),
            dma((3, n_table)),
            dma((4, n_rep)),
            dma((4, n_rep)),
            dma((n_rep,)),
            dma((n_rep,)),
            dma((n_table,)),
            dma((n_table,)),
            dma((n_rep,)),
            dma((n_rep,)),
            dma((n_table,)),
            dma((n_table,)),
            dma((n_rep,)),
            dma((n_rep,)),
        ],
        compiler_params=pltpu.CompilerParams(
            collective_id=0, has_side_effects=True, vmem_limit_bytes=56 * 1024 * 1024
        ),
        name="edge_window",
    )(
        cold_table,
        cold_state[:, None],
        hot_table,
        hot_state[:, None],
        relations,
        head_owner,
        head_row[None, :],
        edge_rel[None, :],
        edge_tail[None, :],
        neg_ids.reshape(-1, 1),
    )
    return (outs[0], outs[1][:, 0], outs[2], outs[3][:, 0])


def pick_plan(*args):
    n_rep, n_table = lax.axis_size("rep"), lax.axis_size("table")
    cold_table, hot_table, relations, head_row, neg_ids = args[0], args[2], args[4], args[6], args[9]
    if fits_kernel(
        n_rep,
        n_table,
        cold_table.shape[0],
        hot_table.shape[0],
        head_row.shape[0],
        neg_ids.shape[1],
        cold_table.shape[1],
        relations.shape[0],
    ):
        return per_device_kernel(*args)
    return per_device(*args)


def solution(mesh):
    in_specs = (
        P("table", None),
        P("table"),
        P("table", None),
        P("table"),
        P(),
        P(("rep", "table"), None),
        P(("rep", "table")),
        P(("rep", "table")),
        P(("rep", "table")),
        P("rep", "table"),
    )
    out_specs = (P("table", None), P("table"), P("table", None), P("table"))
    return jax.shard_map(
        pick_plan, mesh=mesh, in_specs=in_specs, out_specs=out_specs, check_vma=False
    )
```

```python
import functools

import jax
import jax.numpy as jnp
from jax import lax
from jax.experimental import pallas as pl
from jax.experimental.pallas import tpu as pltpu
from jax.sharding import PartitionSpec as P

learn_rate = 0.5


def with_relation(relation, vector):
    half_width = vector.shape[1] // 2
    v_re, v_im = (vector[:, :half_width], vector[:, half_width:])
    r_re, r_im = (relation[:, :half_width], relation[:, half_width:])
    return jnp.concatenate([v_re * r_re - v_im * r_im, v_re * r_im + v_im * r_re], axis=1)


def against_relation(relation, vector):
    half_width = vector.shape[1] // 2
    v_re, v_im = (vector[:, :half_width], vector[:, half_width:])
    r_re, r_im = (relation[:, :half_width], relation[:, half_width:])
    return jnp.concatenate([r_re * v_re + r_im * v_im, r_re * v_im - r_im * v_re], axis=1)


def edge_terms(head_vec, relation, tail_vec, negatives, live_mask):
    contract = (((1,), (1,)), ((), ()))
    across = (((0,), (0,)), ((), ()))
    head_f = head_vec.astype(jnp.float32)
    tail_f = tail_vec.astype(jnp.float32)
    queries = with_relation(relation, head_f)
    probes = against_relation(relation, tail_f)
    positive = jnp.sum(queries * tail_f, axis=1)
    query_b = queries.astype(jnp.bfloat16)
    probe_b = probes.astype(jnp.bfloat16)
    tail_scores = lax.dot_general(query_b, negatives, contract, preferred_element_type=jnp.float32)
    head_scores = lax.dot_general(probe_b, negatives, contract, preferred_element_type=jnp.float32)
    pos_weight = -jax.nn.sigmoid(-positive) * live_mask
    tail_weight = (jax.nn.sigmoid(tail_scores) * live_mask[:, None]).astype(jnp.bfloat16)
    head_weight = (jax.nn.sigmoid(head_scores) * live_mask[:, None]).astype(jnp.bfloat16)
    tail_mix = jnp.dot(tail_weight, negatives, preferred_element_type=jnp.float32)
    head_mix = jnp.dot(head_weight, negatives, preferred_element_type=jnp.float32)
    head_grad = against_relation(relation, pos_weight[:, None] * tail_f + tail_mix).astype(
        jnp.bfloat16
    )
    tail_grad = with_relation(relation, pos_weight[:, None] * head_f + head_mix)
    neg_grad = lax.dot_general(
        tail_weight, query_b, across, preferred_element_type=jnp.float32
    ) + lax.dot_general(head_weight, probe_b, across, preferred_element_type=jnp.float32)
    return (head_grad, tail_grad, neg_grad)


def adagrad(weights, state, grad):
    new_state = state + jnp.mean(grad * grad, axis=1)
    return (weights - learn_rate * grad / jnp.sqrt(new_state)[:, None], new_state)


def per_device(
    cold_table,
    cold_state,
    hot_table,
    hot_state,
    relations,
    head_owner,
    head_row,
    edge_rel,
    edge_tail,
    neg_ids,
):
    n_table = lax.axis_size("table")
    edge_count = head_row.shape[0]
    capacity = 2 * edge_count // n_table
    slot_total = n_table * capacity
    feature_width = cold_table.shape[1]
    cold_bf = cold_table.astype(jnp.bfloat16)
    hot_bf = hot_table.astype(jnp.bfloat16)
    local_negs = cold_bf[neg_ids[0]]
    hot_all, negatives = (
        lax.all_gather(hot_bf, "table", axis=0, tiled=True),
        lax.all_gather(local_negs, "table", axis=0, tiled=True),
    )
    owners = head_owner[:, 0]
    onehot = (owners[:, None] == jnp.arange(n_table, dtype=jnp.int32)[None, :]).astype(jnp.int32)
    position = jnp.arange(edge_count)
    before = (position[:, None] > position[None, :]).astype(jnp.bfloat16)
    counts = jnp.dot(before, onehot.astype(jnp.bfloat16), preferred_element_type=jnp.float32)
    slot_rank = jnp.sum(counts.astype(jnp.int32) * onehot, axis=1)
    slot_ids = owners * capacity + slot_rank
    cold_grad = jnp.zeros(cold_table.shape, jnp.float32)
    records = jnp.stack([head_row, edge_rel, edge_tail, jnp.ones_like(head_row)])
    packed = jnp.zeros((4, slot_total), jnp.int32).at[:, slot_ids].set(records)
    arrived = lax.all_to_all(
        packed.reshape(4, n_table, capacity), "table", split_axis=1, concat_axis=1, tiled=True
    )
    arrived = arrived.reshape(4, slot_total)
    row_ids, rel_ids, tail_ids, live_ids = (arrived[0], arrived[1], arrived[2], arrived[3])
    tail_live = live_ids.astype(jnp.float32)
    head_grad, tail_grad, neg_grad = edge_terms(
        cold_bf[row_ids], relations[rel_ids], hot_all[tail_ids], negatives, tail_live
    )
    cold_grad = cold_grad.at[row_ids].add(head_grad.astype(jnp.float32))
    hot_grad = jnp.zeros((hot_all.shape[0], feature_width), jnp.float32).at[tail_ids].add(tail_grad)
    hot_share, neg_share = (
        lax.psum_scatter(hot_grad, "table", scatter_dimension=0, tiled=True),
        lax.psum_scatter(neg_grad, "table", scatter_dimension=0, tiled=True),
    )
    cold_grad = cold_grad.at[neg_ids[0]].add(neg_share)
    cold_total, hot_total = lax.psum((cold_grad, hot_share), "rep")
    new_cold_table, new_cold_state = adagrad(cold_table, cold_state, cold_total)
    new_hot_table, new_hot_state = adagrad(hot_table, hot_state, hot_total)
    return (new_cold_table, new_cold_state, new_hot_table, new_hot_state)


def fits_kernel(n_rep, n_table, cold_rows, hot_rows, edges, neg_dev, width, rel_count):
    quarter = hot_rows // n_rep
    sizes = (n_rep, n_table, cold_rows, hot_rows, edges)
    return (
        all(s & (s - 1) == 0 for s in sizes)
        and 2 * edges // n_table == 128
        and n_table % 4 == 0
        and quarter % 16 == 0
        and quarter <= 256
        and neg_dev == 8
        and cold_rows % 256 == 0
        and cold_rows <= 4096
        and width % 2 == 0
        and width <= 512
        and n_table * hot_rows <= 4096
        and rel_count <= 1024
    )


def edge_kernel(
    dims,
    cold_ref,
    cstate_ref,
    hot_ref,
    hstate_ref,
    rel_ref,
    owner_ref,
    hrow_ref,
    erel_ref,
    etail_ref,
    nid_ref,
    cold_out,
    cstate_out,
    hot_out,
    hstate_out,
    coldbf,
    relparts,
    outbox,
    ids,
    hotall,
    negall,
    negbf,
    nidall,
    rowids,
    hgrad,
    hotgrad,
    hotrecv,
    hotsum,
    hotrecv2,
    hotfin,
    neggrad,
    negrecv,
    negfin,
    send1,
    recv1,
    send2,
    recv2,
    send3,
    recv3,
    send4,
    recv4,
    send5,
    recv5,
    send6,
    recv6,
    send7,
    recv7,
):
    n_rep, n_table = dims
    f32, bf16, i32 = jnp.float32, jnp.bfloat16, jnp.int32
    rep, tab = lax.axis_index("rep"), lax.axis_index("table")
    rows_c, width = cold_ref.shape
    half = width // 2
    edges = owner_ref.shape[0]
    rows_h = hot_ref.shape[0]
    quarter = rows_h // n_rep
    hot_total = n_table * rows_h
    rel_count = rel_ref.shape[0]
    padw = 256
    full = 2 * padw

    def spread(v):
        pad = jnp.zeros((v.shape[0], padw - half), v.dtype)
        return jnp.concatenate([v[:, :half], pad, v[:, half:], pad], axis=1)

    def close(v):
        return jnp.concatenate([v[:, :half], v[:, padw : padw + half]], axis=1)

    def dot(a, b, ca=1, cb=0):
        return lax.dot_general(a, b, (((ca,), (cb,)), ((), ())), preferred_element_type=f32)

    def hot_one(cond):
        return jnp.where(cond, 1.0, 0.0).astype(bf16)

    def to_table(step):
        return (rep, lax.rem(tab + step, n_table))

    def to_rep(step):
        return (lax.rem(rep + step, n_rep), tab)

    def remote(src, dst, ss, rs, dev):
        return pltpu.make_async_remote_copy(
            src_ref=src,
            dst_ref=dst,
            send_sem=ss,
            recv_sem=rs,
            device_id=dev,
            device_id_type=pl.DeviceIdType.MESH,
        )

    barrier = pltpu.get_barrier_semaphore()
    for s in range(1, n_table):
        pl.semaphore_signal(barrier, 1, device_id=to_table(s), device_id_type=pl.DeviceIdType.MESH)
    for s in range(1, n_rep):
        pl.semaphore_signal(barrier, 1, device_id=to_rep(s), device_id_type=pl.DeviceIdType.MESH)

    mine = hot_ref[pl.ds(pl.multiple_of(rep * quarter, quarter), quarter), :]
    hotall[rep, tab] = spread(mine).astype(bf16)

    owner = owner_ref[...]
    lane = lax.broadcasted_iota(i32, (edges, 128), 1)
    owned = lane == owner
    owned_b = hot_one(owned)
    before = hot_one(
        lax.broadcasted_iota(i32, (edges, edges), 0) > lax.broadcasted_iota(i32, (edges, edges), 1)
    )
    rank = jnp.sum(jnp.where(owned, dot(before, owned_b), 0.0), axis=1, keepdims=True)
    slot = owner * 128 + rank.astype(i32)
    hrow, erel, etail = hrow_ref[...], erel_ref[...], etail_ref[...]
    t_block = etail // rows_h
    t_in = etail % rows_h
    t_group = (t_in // quarter) * n_table + t_block
    fields = [
        hrow // 32,
        hrow % 32,
        erel // 32,
        erel % 32,
        t_group,
        t_in % quarter,
        jnp.ones_like(hrow),
        jnp.zeros_like(hrow),
    ]
    records = jnp.concatenate([f.astype(f32) for f in fields], axis=0).astype(bf16)
    for o in range(n_table):
        place = hot_one(lane + o * 128 == slot)
        outbox[o] = dot(records, place)
    pl.semaphore_wait(barrier, n_table + n_rep - 2)
    ids[rep, tab] = outbox[tab]

    first = []
    for s in range(1, n_table):
        dev = to_table(s)
        first.append(remote(outbox.at[dev[1]], ids.at[rep, tab], send1.at[0, s], recv1.at[0, s], dev))
        first.append(remote(hotall.at[rep, tab], hotall.at[rep, tab], send1.at[1, s], recv1.at[1, s], dev))
    for c in first:
        c.start()

    coldbf[...] = spread(cold_ref[...]).astype(bf16)
    nid = nid_ref[...]
    pick = hot_one(lax.broadcasted_iota(i32, (8, rows_c), 1) == nid)
    negall[rep, tab] = dot(pick, coldbf[...])
    nidall[rep] = jnp.broadcast_to(nid.astype(f32), (8, 128))
    more = []
    for s in range(1, n_table):
        more.append(
            remote(negall.at[rep, tab], negall.at[rep, tab], send1.at[2, s], recv1.at[2, s], to_table(s))
        )
    for c in more:
        c.start()

    rel = spread(rel_ref[...])
    rel_a = rel.astype(bf16)
    rest = rel - rel_a.astype(f32)
    rel_b = rest.astype(bf16)
    relparts[0] = rel_a
    relparts[1] = rel_b
    relparts[2] = (rest - rel_b.astype(f32)).astype(bf16)
    hotgrad[...] = jnp.zeros_like(hotgrad)
    neggrad[...] = jnp.zeros_like(neggrad)

    for c in first + more:
        c.wait()

    second = []
    for s in range(1, n_rep):
        dev = to_rep(s)
        second.append(remote(hotall.at[rep], hotall.at[rep], send2.at[0, s], recv2.at[0, s], dev))
        second.append(remote(ids.at[rep], ids.at[rep], send2.at[1, s], recv2.at[1, s], dev))
        second.append(remote(negall.at[rep], negall.at[rep], send2.at[2, s], recv2.at[2, s], dev))
        second.append(remote(nidall.at[rep], nidall.at[rep], send2.at[3, s], recv2.at[3, s], dev))
    for c in second:
        c.start()
    for c in second:
        c.wait()
    negbf[...] = negall[...].reshape(n_rep, n_table * 8, full).astype(bf16)

    def with_rel(r, v):
        r_re, r_im, v_re, v_im = r[:, :padw], r[:, padw:], v[:, :padw], v[:, padw:]
        return jnp.concatenate([v_re * r_re - v_im * r_im, v_re * r_im + v_im * r_re], axis=1)

    def against_rel(r, v):
        r_re, r_im, v_re, v_im = r[:, :padw], r[:, padw:], v[:, :padw], v[:, padw:]
        return jnp.concatenate([r_re * v_re + r_im * v_im, r_re * v_im - r_im * v_re], axis=1)

    chunk = 512
    per = n_table * 128 // chunk

    def edges_of(q, own):
        def body(c, carry):
            f = jnp.concatenate([ids[q, 4 * c + i] for i in range(4)], axis=1)
            g = f.T.astype(i32)
            f = f.astype(i32)
            row_row = f[0:1] * 32 + f[1:2]
            rowids[q, c] = row_row
            row_col = g[:, 0:1] * 32 + g[:, 1:2]
            rel_col = g[:, 2:3] * 32 + g[:, 3:4]
            tail_col = g[:, 4:5] * quarter + g[:, 5:6]
            live = g[:, 6:7].astype(f32)
            wide = lambda n: lax.broadcasted_iota(i32, (chunk, n), 1)
            head_v = dot(hot_one(wide(rows_c) == row_col), coldbf[...])
            tail_v = dot(hot_one(wide(hot_total) == tail_col), hotall[...].reshape(hot_total, full))
            pick_r = hot_one(wide(rel_count) == rel_col)
            r = dot(pick_r, relparts[0]) + dot(pick_r, relparts[1]) + dot(pick_r, relparts[2])
            neg = negbf[q]
            queries = with_rel(r, head_v)
            positive = jnp.sum(queries * tail_v, axis=1, keepdims=True)
            query_b = queries.astype(bf16)
            tail_w = (jax.nn.sigmoid(dot(query_b, neg, 1, 1)) * live).astype(bf16)
            pos_w = -jax.nn.sigmoid(-positive) * live
            hgrad[q, c] = against_rel(r, pos_w * tail_v + dot(tail_w, neg)).astype(bf16)
            if own:
                probe_b = against_rel(r, tail_v).astype(bf16)
                head_w = (jax.nn.sigmoid(dot(probe_b, neg, 1, 1)) * live).astype(bf16)
                tail_g = with_rel(r, pos_w * head_v + dot(head_w, neg))
                neg_g = dot(tail_w, query_b, 0, 0) + dot(head_w, probe_b, 0, 0)
                neggrad[...] += neg_g.reshape(n_table, 8, full)
                hi = tail_g.astype(bf16)
                lo = (tail_g - hi.astype(f32)).astype(bf16)
                tail_row = f[4:5] * quarter + f[5:6]
                put = hot_one(lax.broadcasted_iota(i32, (hot_total, chunk), 0) == tail_row)
                hotgrad[...] += (dot(put, hi) + dot(put, lo)).reshape(hotgrad.shape)
            return carry

        lax.fori_loop(0, per, body, 0)

    edges_of(rep, True)

    third = []
    for s in range(1, n_rep):
        dev = to_rep(s)
        third.append(remote(hotgrad.at[dev[0]], hotrecv.at[rep], send3.at[s], recv3.at[s], dev))
    for s in range(1, n_table):
        dev = to_table(s)
        third.append(remote(neggrad.at[dev[1]], negrecv.at[tab], send6.at[s], recv6.at[s], dev))
    for c in third:
        c.start()
    hotrecv[rep] = hotgrad[rep]
    negrecv[tab] = neggrad[tab]

    others = [lax.rem(rep + s, n_rep) for s in range(1, n_rep)]
    split = max(1, len(others) // 3)
    for q in others[:split]:
        edges_of(q, False)

    for c in third:
        c.wait()
    acc = hotrecv[0]
    for k in range(1, n_rep):
        acc = acc + hotrecv[k]
    hotsum[...] = acc
    nacc = negrecv[0]
    for k in range(1, n_table):
        nacc = nacc + negrecv[k]
    negfin[rep] = nacc
    fourth = []
    for s in range(1, n_table):
        dev = to_table(s)
        fourth.append(remote(hotsum.at[dev[1]], hotrecv2.at[tab], send4.at[s], recv4.at[s], dev))
    for s in range(1, n_rep):
        fourth.append(remote(negfin.at[rep], negfin.at[rep], send7.at[s], recv7.at[s], to_rep(s)))
    for c in fourth:
        c.start()
    hotrecv2[tab] = hotsum[tab]

    for q in others[split : 2 * split]:
        edges_of(q, False)

    for c in fourth:
        c.wait()
    acc = hotrecv2[0]
    for k in range(1, n_table):
        acc = acc + hotrecv2[k]
    hotfin[rep] = acc
    fifth = [remote(hotfin.at[rep], hotfin.at[rep], send5.at[s], recv5.at[s], to_rep(s)) for s in range(1, n_rep)]
    for c in fifth:
        c.start()

    for q in others[2 * split :]:
        edges_of(q, False)

    def step(weights, state, grad):
        new_state = state + jnp.sum(grad * grad, axis=1, keepdims=True) / width
        return weights - learn_rate * close(grad) / jnp.sqrt(new_state), new_state

    def column(v):
        return jnp.broadcast_to(v, (8, v.shape[1])).T[:, :1]

    def line(v):
        return jnp.broadcast_to(v, (v.shape[0], 128)).T[:1]

    neg_total = negfin[...].reshape(n_rep * 8, full)
    neg_hi = neg_total.astype(bf16)
    neg_rest = neg_total - neg_hi.astype(f32)
    neg_mid = neg_rest.astype(bf16)
    neg_lo = (neg_rest - neg_mid.astype(f32)).astype(bf16)
    neg_col = nidall[...].reshape(n_rep * 8, 128).astype(i32)[:, :1]
    block = 256

    def finish(b, carry):
        start = pl.multiple_of(b * block, block)
        base = lax.broadcasted_iota(i32, (block, chunk), 0) + start
        grad = jnp.zeros((block, full), f32)
        for q in range(n_rep):
            for c in range(per):
                grad = grad + dot(hot_one(base == rowids[q, c]), hgrad[q, c])
        put = hot_one(lax.broadcasted_iota(i32, (n_rep * 8, block), 1) + start == neg_col)
        grad = grad + (dot(put, neg_hi, 0, 0) + dot(put, neg_mid, 0, 0) + dot(put, neg_lo, 0, 0))
        at = pl.ds(start, block)
        table, state = step(cold_ref[at, :], column(cstate_ref[:, at]), grad)
        cold_out[at, :] = table
        cstate_out[:, at] = line(state)
        return carry

    lax.fori_loop(0, rows_c // block, finish, 0)

    for c in fifth:
        c.wait()
    table, state = step(hot_ref[...], column(hstate_ref[...]), hotfin[...].reshape(rows_h, full))
    hot_out[...] = table
    hstate_out[...] = line(state)


def per_device_kernel(
    cold_table,
    cold_state,
    hot_table,
    hot_state,
    relations,
    head_owner,
    head_row,
    edge_rel,
    edge_tail,
    neg_ids,
):
    n_rep, n_table = lax.axis_size("rep"), lax.axis_size("table")
    rows_c, width = cold_table.shape
    rows_h = hot_table.shape[0]
    edges = head_row.shape[0]
    rel_count = relations.shape[0]
    quarter = rows_h // n_rep
    full, chunk = 512, 512
    per = n_table * 128 // chunk
    f32, bf16 = jnp.float32, jnp.bfloat16
    dma = pltpu.SemaphoreType.DMA
    vmem = pl.BlockSpec(memory_space=pltpu.VMEM)
    outs = pl.pallas_call(
        functools.partial(edge_kernel, (n_rep, n_table)),
        out_shape=[
            jax.ShapeDtypeStruct((rows_c, width), f32),
            jax.ShapeDtypeStruct((1, rows_c), f32),
            jax.ShapeDtypeStruct((rows_h, width), f32),
            jax.ShapeDtypeStruct((1, rows_h), f32),
        ],
        in_specs=[vmem] * 10,
        out_specs=[vmem] * 4,
        scratch_shapes=[
            pltpu.VMEM((rows_c, full), bf16),
            pltpu.VMEM((3, rel_count, full), bf16),
            pltpu.VMEM((n_table, 8, 128), f32),
            pltpu.VMEM((n_rep, n_table, 8, 128), f32),
            pltpu.VMEM((n_rep, n_table, quarter, full), bf16),
            pltpu.VMEM((n_rep, n_table, 8, full), f32),
            pltpu.VMEM((n_rep, n_table * 8, full), bf16),
            pltpu.VMEM((n_rep, 8, 128), f32),
            pltpu.VMEM((n_rep, per, 1, chunk), jnp.int32),
            pltpu.VMEM((n_rep, per, chunk, full), bf16),
            pltpu.VMEM((n_rep, n_table, quarter, full), f32),
            pltpu.VMEM((n_rep, n_table, quarter, full), f32),
            pltpu.VMEM((n_table, quarter, full), f32),
            pltpu.VMEM((n_table, quarter, full), f32),
            pltpu.VMEM((n_rep, quarter, full), f32),
            pltpu.VMEM((n_table, 8, full), f32),
            pltpu.VMEM((n_table, 8, full), f32),
            pltpu.VMEM((n_rep, 8, full), f32),
            dma((3, n_table)),
            dma((3, n_table)),
            dma((4, n_rep)),
            dma((4, n_rep)),
            dma((n_rep,)),
            dma((n_rep,)),
            dma((n_table,)),
            dma((n_table,)),
            dma((n_rep,)),
            dma((n_rep,)),
            dma((n_table,)),
            dma((n_table,)),
            dma((n_rep,)),
            dma((n_rep,)),
        ],
        compiler_params=pltpu.CompilerParams(
            collective_id=0, has_side_effects=True, vmem_limit_bytes=56 * 1024 * 1024
        ),
        name="edge_window",
    )(
        cold_table,
        cold_state[None, :],
        hot_table,
        hot_state[None, :],
        relations,
        head_owner,
        head_row[None, :],
        edge_rel[None, :],
        edge_tail[None, :],
        neg_ids.reshape(-1, 1),
    )
    return (outs[0], outs[1][0], outs[2], outs[3][0])


def pick_plan(*args):
    n_rep, n_table = lax.axis_size("rep"), lax.axis_size("table")
    cold_table, hot_table, relations, head_row, neg_ids = args[0], args[2], args[4], args[6], args[9]
    if fits_kernel(
        n_rep,
        n_table,
        cold_table.shape[0],
        hot_table.shape[0],
        head_row.shape[0],
        neg_ids.shape[1],
        cold_table.shape[1],
        relations.shape[0],
    ):
        return per_device_kernel(*args)
    return per_device(*args)


def solution(mesh):
    in_specs = (
        P("table", None),
        P("table"),
        P("table", None),
        P("table"),
        P(),
        P(("rep", "table"), None),
        P(("rep", "table")),
        P(("rep", "table")),
        P(("rep", "table")),
        P("rep", "table"),
    )
    out_specs = (P("table", None), P("table"), P("table", None), P("table"))
    return jax.shard_map(
        pick_plan, mesh=mesh, in_specs=in_specs, out_specs=out_specs, check_vma=False
    )
```
